32 devices in a mesh: xy: 16 (over z, x, core), gz: 2 (over y).
Axes of the slice: x: 2, y: 2, z: 4, core: 2. Of those that a mesh axis runs over, the one named last changes fastest.
Arguments:
- previous: float32 [256, 128, 256], P('xy', 'gz'), may hold values from -2.1 to 2.1
- current: float32 [256, 128, 256], P('xy', 'gz'), may hold values from -1.8 to 1.8
- stiffness: float32 [256, 128, 256], P('xy', 'gz'), may hold values from 0.05 to 0.2
- buoyancy: float32 [256, 128, 256], P('xy', 'gz'), may hold values from 0.5 to 1
Outputs:
- next_field: float32 [256, 128, 256], P('xy', 'gz')
- coefficients: float32 [128, 64, 128], P(('xy', 'gz'))
The draws below stay inside these ranges and needn't reach their ends.
All inputs are finite; a program needn't handle non-finite values.
Results may differ from the reference program's by a relative error of at most 0.00002.
Values sent between devices are 32-bit elements; how exact they have to be, the bound alone decides.
A program may use at most 64 MiB of HBM per device.

```python
import math
import jax
import jax.numpy as jnp
from jax import lax

NY = 256
NX = 256
NZ = 128


def wave_parts(key):
    array_shape = (NX, NZ, NY)
    normal_part = jax.random.normal(jax.random.fold_in(key, 11), array_shape, jnp.float32)
    place_x = lax.broadcasted_iota(jnp.int32, (NX, 1, 1), 0)
    place_z = lax.broadcasted_iota(jnp.int32, (1, NZ, 1), 1)
    place_y = lax.broadcasted_iota(jnp.int32, (1, 1, NY), 2)
    parity = (place_x + place_z + place_y) % 2
    alternate = 1.0 - 2.0 * parity.astype(jnp.float32)
    return (alternate, normal_part)


def draw_current(key, part):
    alternate, normal_part = wave_parts(key)
    amount = 1.0 + 0.25 * jnp.clip(normal_part, -2.0, 2.0)
    return (alternate * amount).astype(jnp.float32)


def draw_previous(key, part):
    alternate, normal_part = wave_parts(key)
    key = jax.random.fold_in(key, 5)
    array_shape = (NX, NZ, NY)
    amount = 1.0 + 0.25 * jnp.clip(normal_part, -2.0, 2.0)
    step_part = 0.2 * jnp.clip(jax.random.normal(key, array_shape, jnp.float32), -3.0, 3.0)
    return (alternate * amount + step_part).astype(jnp.float32)


def block_levels(key, shape, split, low, largest):
    gain = 1.0
    for axis_at, shards_of in split:
        draws = jax.random.uniform(jax.random.fold_in(jax.random.fold_in(key, 6), axis_at), (shards_of,), jnp.float32, low / len(split), largest / len(split))
        gain = gain * jnp.repeat(jnp.exp(draws), shape[axis_at] // shards_of).reshape((-1,) + (1,) * (len(shape) - 1 - axis_at))
    return gain


def setup_inputs(seed: int = 0) -> dict:
    keys = jax.random.split(jax.random.key(seed), 5)
    previous = draw_previous(jax.random.fold_in(keys[4], 71), 0)
    current = draw_current(jax.random.fold_in(keys[4], 71), 0)
    stiffness = jnp.clip(jnp.exp(math.log(0.2) - 1.3862944 * jax.random.uniform(keys[2], (NX, NZ, NY), jnp.float32) ** block_levels(keys[2], (NX, NZ, NY), ((0, 16), (1, 2)), -0.2, 0.2)), 0.05, 0.2)
    buoyancy = jnp.clip(jnp.exp(math.log(1.0) - 0.6931472 * jax.random.uniform(keys[3], (NX, NZ, NY), jnp.float32) ** block_levels(keys[3], (NX, NZ, NY), ((0, 16), (1, 2)), -0.2, 0.2)), 0.5, 1.0)
    return {"previous": previous, "current": current, "stiffness": stiffness, "buoyancy": buoyancy}


coeffs = (1225.0 / 1024.0, -245.0 / 3072.0, 49.0 / 5120.0, -5.0 / 7168.0)
alpha_lift = -1.586134342
beta_lift = -0.05298011854
gamma_lift = 0.8829110762
delta_lift = 0.4435068522
wavelet_scale = 1.149604398


def cut_along(source, begin_at, length, sweep_direction):
    return lax.slice_in_dim(source, begin_at, begin_at + length, axis=sweep_direction)


def compute_flux(padded, bpadded, sweep_direction, margin, first_face, end_face, first_global, extent):
    length = end_face - first_face
    gradient = None
    for term_index, weight in enumerate(coeffs):
        offset = term_index + 1
        summand = weight * (cut_along(padded, first_face + offset + margin, length, sweep_direction) - cut_along(padded, first_face + 1 - offset + margin, length, sweep_direction))
        gradient = summand if gradient is None else gradient + summand
    face_buoy = 0.5 * (cut_along(bpadded, first_face + margin, length, sweep_direction) + cut_along(bpadded, first_face + 1 + margin, length, sweep_direction))
    face_ids = lax.broadcasted_iota(jnp.int32, gradient.shape, sweep_direction) + first_face + first_global
    inside = (face_ids >= 0) & (face_ids <= extent - 2)
    return jnp.where(inside, face_buoy * gradient, jnp.float32(0.0))


def diverge(flux_faces, sweep_direction, length):
    result = None
    for term_index, weight in enumerate(coeffs):
        offset = term_index + 1
        summand = weight * (cut_along(flux_faces, offset + 3, length, sweep_direction) - cut_along(flux_faces, 4 - offset, length, sweep_direction))
        result = summand if result is None else result + summand
    return result


def divergence(field, buoyancy, sweep_direction):
    length = field.shape[sweep_direction]
    widths = [(0, 0), (0, 0), (0, 0)]
    widths[sweep_direction] = (8, 8)
    padded = jnp.pad(field, widths)
    bpadded = jnp.pad(buoyancy, widths)
    flux_faces = compute_flux(padded, bpadded, sweep_direction, 8, -4, length + 4, 0, length)
    return diverge(flux_faces, sweep_direction, length)


def shift_next(sample_values, sweep_direction):
    length = sample_values.shape[sweep_direction]
    return jnp.concatenate([cut_along(sample_values, 1, length - 1, sweep_direction), cut_along(sample_values, length - 1, 1, sweep_direction)], axis=sweep_direction)


def shift_prev(sample_values, sweep_direction):
    length = sample_values.shape[sweep_direction]
    return jnp.concatenate([cut_along(sample_values, 0, 1, sweep_direction), cut_along(sample_values, 0, length - 1, sweep_direction)], axis=sweep_direction)


def lift_line(sample_values, sweep_direction):
    length = sample_values.shape[sweep_direction]
    even_samples = lax.slice_in_dim(sample_values, 0, length, 2, axis=sweep_direction)
    odd_samples = lax.slice_in_dim(sample_values, 1, length, 2, axis=sweep_direction)
    odd_samples = odd_samples + alpha_lift * (even_samples + shift_next(even_samples, sweep_direction))
    even_samples = even_samples + beta_lift * (shift_prev(odd_samples, sweep_direction) + odd_samples)
    odd_samples = odd_samples + gamma_lift * (even_samples + shift_next(even_samples, sweep_direction))
    even_samples = even_samples + delta_lift * (shift_prev(odd_samples, sweep_direction) + odd_samples)
    return jnp.stack((even_samples * wavelet_scale, odd_samples / wavelet_scale), axis=sweep_direction + 1).reshape(sample_values.shape)


def plane_levels(snapshot):
    sample_values = lift_line(snapshot, 0)
    sample_values = lift_line(sample_values, 2)
    corner = sample_values[::2, :, ::2]
    corner = lift_line(lift_line(corner, 0), 2)
    return sample_values.at[::2, :, ::2].set(corner)


def depth_levels(sample_values):
    for depth_level in range(4):
        stride = 2 ** depth_level
        portion = sample_values[:, ::stride, :]
        sample_values = sample_values.at[:, ::stride, :].set(lift_line(portion, 1))
    return sample_values


def reference(previous, current, stiffness, buoyancy):
    laplace_sum = divergence(current, buoyancy, 0) + divergence(current, buoyancy, 1) + divergence(current, buoyancy, 2)
    next_field = 2.0 * current - previous + stiffness * laplace_sum
    snapshot = next_field[::2, ::2, ::2]
    return next_field, depth_levels(plane_levels(snapshot))
```

```python
import functools

import jax
import jax.numpy as jnp
import numpy as np
from jax import lax
from jax.experimental import pallas as pl
from jax.experimental.pallas import tpu as pltpu
from jax.sharding import PartitionSpec as P

coeffs = (1225.0 / 1024.0, -245.0 / 3072.0, 49.0 / 5120.0, -5.0 / 7168.0)
alpha_lift = -1.586134342
beta_lift = -0.05298011854
gamma_lift = 0.8829110762
delta_lift = 0.4435068522
wavelet_scale = 1.149604398

UP_ROWS = (0, 2, 4, 6, 1)
DOWN_ROWS = (0, 2, 4, 6, 5, 7)
UP2_ROWS = (0,)
DOWN2_ROWS = (4, 6)
CHUNK = 16
HALO = 8
HIGHEST = lax.Precision.HIGHEST


def lift_rows(v):
    s, d = v[0::2].copy(), v[1::2].copy()
    nxt = lambda a: np.concatenate([a[1:], a[-1:]])
    prv = lambda a: np.concatenate([a[:1], a[:-1]])
    d = d + alpha_lift * (s + nxt(s))
    s = s + beta_lift * (prv(d) + d)
    d = d + gamma_lift * (s + nxt(s))
    s = s + delta_lift * (prv(d) + d)
    out = np.empty_like(v)
    out[0::2], out[1::2] = s * wavelet_scale, d / wavelet_scale
    return out


def two_level(n):
    one = lift_rows(np.eye(n))
    two = one.copy()
    two[0::2] = lift_rows(one[0::2])
    return one, two


def x_table(strips, rows):
    one, two = two_level(strips * rows)
    table = []
    for at in (0, 1, 2, strips - 2, strips - 1):
        entry = []
        for step, wanted in ((0, range(rows)), (1, UP_ROWS), (-1, DOWN_ROWS), (2, UP2_ROWS), (-2, DOWN2_ROWS)):
            for row in wanted:
                to = (at + step) * rows + row
                inside = 0 <= at + step < strips
                for source in range(at * rows, (at + 1) * rows):
                    entry += [two[to, source], one[to, source]] if inside else [0.0, 0.0]
        table.append(entry)
    return np.asarray(table, np.float32)


def y_matrices(n):
    grad = np.zeros((n, n))
    div = np.zeros((n, n))
    for k, c in enumerate(coeffs, 1):
        for j in range(n - 1):
            if j + k < n:
                grad[j + k, j] += c
            if j + 1 - k >= 0:
                grad[j + 1 - k, j] -= c
        for i in range(n):
            if i + k - 1 <= n - 2:
                div[i + k - 1, i] += c
            if i - k >= 0:
                div[i - k, i] -= c
    one, two = two_level(n // 2)
    two[1::2] = one[1::2]
    lift = np.zeros((n, n))
    lift[0::2, : n // 2] = one.T
    lift[0::2, n // 2 :] = two.T
    return grad.astype(np.float32), div.astype(np.float32), lift.astype(np.float32)


def z_matrix(n):
    w = np.eye(n)
    for level in range(4):
        w[:: 2**level] = lift_rows(w[:: 2**level])
    return w.astype(np.float32)


def kernel(
    strips, slabs,
    cur, prev, stiff, buoy, tab, gy, dy, ly, wz,
    next_out, coef_out,
    cp, bp, fx, acc, pv, sv, nf, gv, dv, lv, wv, con, up, down, up2, down2, zfull,
    lsem, ssem, rsem, zssem, zrsem, gssem, grsem,
):
    p, g = lax.axis_index("xy"), lax.axis_index("gz")
    X, Z, Y = cur.shape
    NC = Z // CHUNK
    HX, HC = X // 2, CHUNK // 2
    part = HX // slabs
    has_l, has_r = p > 0, p < strips - 1
    has_ll, has_rr = p > 1, p < strips - 2
    has_b, has_t = g > 0, g < slabs - 1
    near = ((has_l, p - 1), (has_r, p + 1), (has_ll, p - 2), (has_rr, p + 2))

    def local(src, dst, k):
        return pltpu.make_async_copy(src, dst, lsem.at[k])

    body = pl.ds(HALO, Z)
    loads = [
        local(cur, cp.at[pl.ds(3, X), body], 0),
        local(buoy, bp.at[pl.ds(0, X), body], 1),
        local(gy, gv, 2),
        local(dy, dv, 3),
        local(prev, pv, 4),
        local(stiff, sv, 5),
        local(ly, lv, 6),
        local(wz, wv, 7),
    ]
    for c in loads:
        c.start()

    barrier = pltpu.get_barrier_semaphore()
    for there, q in near:
        @pl.when(there)
        def _():
            pl.semaphore_signal(barrier, inc=1, device_id=(q, g), device_id_type=pl.DeviceIdType.MESH)
    for o in range(1, slabs):
        pl.semaphore_signal(
            barrier, inc=1, device_id=(p, lax.rem(g + o, slabs)), device_id_type=pl.DeviceIdType.MESH
        )

    def zero(ref):
        ref[...] = jnp.zeros(ref.shape, jnp.float32)

    @pl.when(jnp.logical_not(has_l))
    def _():
        zero(cp.at[pl.ds(0, 3), body])
        zero(fx.at[pl.ds(0, 4)])
        zero(up)

    @pl.when(jnp.logical_not(has_r))
    def _():
        zero(cp.at[pl.ds(X + 3, 4), body])
        zero(fx.at[pl.ds(X + 4, 3)])
        zero(down)

    @pl.when(jnp.logical_not(has_ll))
    def _():
        zero(up2)

    @pl.when(jnp.logical_not(has_rr))
    def _():
        zero(down2)

    @pl.when(jnp.logical_not(has_b))
    def _():
        zero(cp.at[pl.ds(3, X), pl.ds(0, HALO)])

    @pl.when(jnp.logical_not(has_t))
    def _():
        zero(cp.at[pl.ds(3, X), pl.ds(HALO + Z, HALO)])

    one = lambda there: there.astype(jnp.int32)
    pl.semaphore_wait(barrier, one(has_l) + one(has_r) + one(has_ll) + one(has_rr) + slabs - 1)

    def remote(src, dst, ss, rs, dev):
        return pltpu.make_async_remote_copy(
            src_ref=src, dst_ref=dst, send_sem=ss, recv_sem=rs, device_id=dev,
            device_id_type=pl.DeviceIdType.MESH,
        )

    def x_copy(kind, c):
        z = pl.ds(c * CHUNK, CHUNK)
        zp = pl.ds(HALO + c * CHUNK, CHUNK)
        sends, q, receives, src, dst = (
            (has_l, p - 1, has_r, cur.at[pl.ds(0, 4), z], cp.at[pl.ds(X + 3, 4), zp]),
            (has_r, p + 1, has_l, cur.at[pl.ds(X - 3, 3), z], cp.at[pl.ds(0, 3), zp]),
            (has_l, p - 1, has_r, buoy.at[pl.ds(0, 1), z], bp.at[pl.ds(X, 1), zp]),
            (has_r, p + 1, has_l, fx.at[pl.ds(X, 4), z], fx.at[pl.ds(0, 4), z]),
            (has_l, p - 1, has_r, fx.at[pl.ds(4, 3), z], fx.at[pl.ds(X + 4, 3), z]),
            (has_r, p + 1, has_l, con.at[c, pl.ds(HX, 5)], up.at[c]),
            (has_l, p - 1, has_r, con.at[c, pl.ds(HX + 5, 6)], down.at[c]),
            (has_rr, p + 2, has_ll, con.at[c, pl.ds(HX + 11, 1)], up2.at[c]),
            (has_ll, p - 2, has_rr, con.at[c, pl.ds(HX + 12, 2)], down2.at[c]),
        )[kind]
        return sends, receives, remote(src, dst, ssem.at[kind, c], rsem.at[kind, c], (q, g))

    def z_copy(kind):
        low, high = pl.ds(0, HALO), pl.ds(Z - HALO, HALO)
        below, above = pl.ds(0, HALO), pl.ds(HALO + Z, HALO)
        sends, q, receives, src, dst = (
            (has_b, g - 1, has_t, cur.at[:, low], cp.at[pl.ds(3, X), above]),
            (has_t, g + 1, has_b, cur.at[:, high], cp.at[pl.ds(3, X), below]),
            (has_b, g - 1, has_t, buoy.at[:, low], bp.at[pl.ds(0, X), above]),
            (has_t, g + 1, has_b, buoy.at[:, high], bp.at[pl.ds(0, X), below]),
        )[kind]
        return sends, receives, remote(src, dst, zssem.at[kind], zrsem.at[kind], (p, q))

    def start(copy):
        sends, _, c = copy
        pl.when(sends)(c.start)

    def arrive(copy):
        _, receives, c = copy
        pl.when(receives)(c.wait_recv)

    def sent(copy):
        sends, _, c = copy
        pl.when(sends)(c.wait_send)

    for c in range(NC):
        for kind in (0, 1, 2):
            start(x_copy(kind, c))
        if c == 0:
            for kind in range(4):
                start(z_copy(kind))

    for c in loads[:4]:
        c.wait()

    rows = 4

    def y_part(i, _):
        x = i * rows
        v = cp[pl.ds(x + 3, rows), HALO : HALO + Z, :].reshape(rows * Z, Y)
        b = bp[pl.ds(x, rows), HALO : HALO + Z, :].reshape(rows * Z, Y)
        grad = jnp.dot(v, gv[...], precision=HIGHEST, preferred_element_type=jnp.float32)
        flux = 0.5 * (b + pltpu.roll(b, Y - 1, 1)) * grad
        acc[pl.ds(x, rows)] = jnp.dot(
            flux, dv[...], precision=HIGHEST, preferred_element_type=jnp.float32
        ).reshape(rows, Z, Y)
        return 0

    lax.fori_loop(0, X // rows, y_part, 0)

    for c in range(NC):
        for kind in (0, 1, 2):
            arrive(x_copy(kind, c))
        zp = slice(HALO + c * CHUNK, HALO + (c + 1) * CHUNK)
        z = slice(c * CHUNK, (c + 1) * CHUNK)

        def x_flux(x, _):
            grad = None
            for k, w in enumerate(coeffs, 1):
                term = w * (cp[x + 3 + k, zp, :] - cp[x + 4 - k, zp, :])
                grad = term if grad is None else grad + term
            flux = 0.5 * (bp[x, zp, :] + bp[x + 1, zp, :]) * grad
            keep = jnp.logical_or(has_r, x < X - 1)
            fx[x + 4, z, :] = jnp.where(keep, flux, 0.0)
            return 0

        lax.fori_loop(0, X, x_flux, 0)
        start(x_copy(3, c))
        start(x_copy(4, c))

    for kind in range(4):
        arrive(z_copy(kind))
    ZP = Z + 2 * HALO
    face = lax.broadcasted_iota(jnp.int32, (ZP, Y), 0) - HALO + g * Z
    inside = jnp.logical_and(face >= 0, face <= slabs * Z - 2)

    def moved(v, k):
        return pltpu.roll(v, (-k) % ZP, 0) if k else v

    def z_part(x, _):
        v, b = cp[x + 3], bp[x]
        grad = None
        for k, w in enumerate(coeffs, 1):
            term = w * (moved(v, k) - moved(v, 1 - k))
            grad = term if grad is None else grad + term
        flux = jnp.where(inside, 0.5 * (b + moved(b, 1)) * grad, 0.0)
        div = None
        for k, w in enumerate(coeffs, 1):
            term = w * (moved(flux, k - 1) - moved(flux, -k))
            div = term if div is None else div + term
        acc[x] = acc[x] + div[HALO : HALO + Z]
        return 0

    lax.fori_loop(0, X, z_part, 0)
    for c in loads[4:7]:
        c.wait()

    even = lax.rem(lax.broadcasted_iota(jnp.int32, (HC, Y // 2), 1), 2) == 0
    kind_of = jnp.minimum(p, 2) + jnp.maximum(p - (strips - 3), 0)
    sent_rows = tuple(range(HX)) + UP_ROWS + DOWN_ROWS + UP2_ROWS + DOWN2_ROWS
    stores = []
    for c in range(NC):
        arrive(x_copy(3, c))
        arrive(x_copy(4, c))
        zp = slice(HALO + c * CHUNK, HALO + (c + 1) * CHUNK)
        z = slice(c * CHUNK, (c + 1) * CHUNK)

        def finish(x, _):
            div = None
            for k, w in enumerate(coeffs, 1):
                term = w * (fx[x + 3 + k, z, :] - fx[x + 4 - k, z, :])
                div = term if div is None else div + term
            value = 2.0 * cp[x + 3, zp, :] - pv[x, z, :] + sv[x, z, :] * (div + acc[x, z, :])
            for h in range(Y // 128):
                nf[h, x, z, :] = value[:, h * 128 : (h + 1) * 128]
            return 0

        lax.fori_loop(0, X, finish, 0)
        for h in range(Y // 128):
            zc = pl.ds(c * CHUNK, CHUNK)
            copy = local(nf.at[h, :, zc], next_out.at[:, zc, pl.ds(h * 128, 128)], 8 + 2 * c + h)
            copy.start()
            stores.append(copy)
        snap = jnp.concatenate(
            [
                jnp.concatenate(
                    [nf[h, 2 * r, pl.ds(c * CHUNK, HC, stride=2), :] for h in range(Y // 128)], axis=1
                )
                for r in range(HX)
            ],
            axis=0,
        )
        t = jnp.dot(snap, lv[...], precision=HIGHEST, preferred_element_type=jnp.float32)
        one_y = [t[r * HC : (r + 1) * HC, : Y // 2] for r in range(HX)]
        two_y = [t[r * HC : (r + 1) * HC, Y // 2 :] for r in range(HX)]
        for at, row in enumerate(sent_rows):
            total = None
            for r in range(HX):
                w2 = tab[kind_of, (at * HX + r) * 2]
                w1 = tab[kind_of, (at * HX + r) * 2 + 1]
                term = jnp.where(even, w2, w1) * two_y[r] if row % 2 == 0 else w1 * one_y[r]
                total = term if total is None else total + term
            con[c, at] = total
        for kind in (5, 6, 7, 8):
            start(x_copy(kind, c))

    def g_copy(o, c):
        to = lax.rem(g + o, slabs)
        mine = pl.ds(pl.multiple_of(g * (Z // 2) + c * HC, HC), HC)
        return remote(
            con.at[c, pl.ds(to * part, part)], zfull.at[:, mine],
            gssem.at[o - 1, c], grsem.at[o - 1, c], (p, to),
        )

    for c in range(NC):
        for kind in (5, 6, 7, 8):
            arrive(x_copy(kind, c))
        for row in range(HX):
            total = con[c, row]
            for ref, wanted in ((up, UP_ROWS), (down, DOWN_ROWS), (up2, UP2_ROWS), (down2, DOWN2_ROWS)):
                if row in wanted:
                    total = total + ref[c, wanted.index(row)]
            con[c, row] = total
        for o in range(1, slabs):
            g_copy(o, c).start()
        zfull[:, pl.ds(pl.multiple_of(g * (Z // 2) + c * HC, HC), HC), :] = con[c, pl.ds(g * part, part)]

    loads[7].wait()
    for c in range(NC):
        for o in range(1, slabs):
            g_copy(o, c).wait_recv()
    for row in range(part):
        coef_out[row] = jnp.dot(
            wv[...], zfull[row], precision=HIGHEST, preferred_element_type=jnp.float32
        )

    for copy in stores:
        copy.wait()
    for kind in range(4):
        sent(z_copy(kind))
    for c in range(NC):
        for kind in range(9):
            sent(x_copy(kind, c))
        for o in range(1, slabs):
            g_copy(o, c).wait_send()


def on_device(strips, slabs, previous, current, stiffness, buoyancy):
    X, Z, Y = current.shape
    NC, HX, HC = Z // CHUNK, X // 2, CHUNK // 2
    depth = slabs * Z // 2
    grad, div, lift = y_matrices(Y)
    hbm = pl.BlockSpec(memory_space=pl.ANY)
    f32 = jnp.float32
    vmem = lambda *shape: pltpu.VMEM(shape, f32)
    dma = lambda *shape: pltpu.SemaphoreType.DMA(shape)
    return pl.pallas_call(
        functools.partial(kernel, strips, slabs),
        out_shape=(
            jax.ShapeDtypeStruct((X, Z, Y), f32),
            jax.ShapeDtypeStruct((HX // slabs, depth, Y // 2), f32),
        ),
        in_specs=[hbm] * 4 + [pl.BlockSpec(memory_space=pltpu.SMEM)] + [hbm] * 4,
        out_specs=(hbm, pl.BlockSpec(memory_space=pltpu.VMEM)),
        scratch_shapes=[
            vmem(X + 7, Z + 2 * HALO, Y),
            vmem(X + 1, Z + 2 * HALO, Y),
            vmem(X + 7, Z, Y),
            vmem(X, Z, Y),
            vmem(X, Z, Y),
            vmem(X, Z, Y),
            vmem(Y // 128, X, Z, 128),
            vmem(Y, Y),
            vmem(Y, Y),
            vmem(Y, Y),
            vmem(depth, depth),
            vmem(NC, HX + 14, HC, Y // 2),
            vmem(NC, 5, HC, Y // 2),
            vmem(NC, 6, HC, Y // 2),
            vmem(NC, 1, HC, Y // 2),
            vmem(NC, 2, HC, Y // 2),
            vmem(HX // slabs, depth, Y // 2),
            dma(8 + 2 * NC),
            dma(9, NC),
            dma(9, NC),
            dma(4),
            dma(4),
            dma(slabs - 1, NC),
            dma(slabs - 1, NC),
        ],
        compiler_params=pltpu.CompilerParams(
            collective_id=0, has_side_effects=True, vmem_limit_bytes=40 * 1024 * 1024
        ),
    )(
        current, previous, stiffness, buoyancy,
        x_table(strips, HX), grad, div, lift, z_matrix(depth),
    )


def solution(mesh):
    return jax.shard_map(
        functools.partial(on_device, mesh.shape["xy"], mesh.shape["gz"]),
        mesh=mesh,
        in_specs=(P("xy", "gz", None),) * 4,
        out_specs=(P("xy", "gz", None), P(("xy", "gz"), None, None)),
        check_vma=False,
    )
```

```python
import functools

import jax
import jax.numpy as jnp
import numpy as np
from jax import lax
from jax.experimental import pallas as pl
from jax.experimental.pallas import tpu as pltpu
from jax.sharding import PartitionSpec as P

coeffs = (1225.0 / 1024.0, -245.0 / 3072.0, 49.0 / 5120.0, -5.0 / 7168.0)
alpha_lift = -1.586134342
beta_lift = -0.05298011854
gamma_lift = 0.8829110762
delta_lift = 0.4435068522
wavelet_scale = 1.149604398

UP_ROWS = (0, 2, 1, (4, 6))
DOWN_ROWS = (4, 6, 5, 7, (0, 2))
UP2_ROWS = (0,)
DOWN2_ROWS = ((4, 6),)
CHUNK = 16
HALO = 8
HIGHEST = lax.Precision.HIGHEST


def lift_rows(v):
    s, d = v[0::2].copy(), v[1::2].copy()
    nxt = lambda a: np.concatenate([a[1:], a[-1:]])
    prv = lambda a: np.concatenate([a[:1], a[:-1]])
    d = d + alpha_lift * (s + nxt(s))
    s = s + beta_lift * (prv(d) + d)
    d = d + gamma_lift * (s + nxt(s))
    s = s + delta_lift * (prv(d) + d)
    out = np.empty_like(v)
    out[0::2], out[1::2] = s * wavelet_scale, d / wavelet_scale
    return out


def two_level(n):
    one = lift_rows(np.eye(n))
    two = one.copy()
    two[0::2] = lift_rows(one[0::2])
    return one, two


def flat(rows):
    return [r for row in rows for r in (row if isinstance(row, tuple) else (row,))]


def x_table(strips, rows):
    one, two = two_level(strips * rows)
    table = []
    for at in (0, 1, 2, strips - 2, strips - 1):
        entry = []
        for step, wanted in ((0, range(rows)), (1, UP_ROWS), (-1, DOWN_ROWS), (2, UP2_ROWS), (-2, DOWN2_ROWS)):
            for row in flat(wanted):
                to = (at + step) * rows + row
                inside = 0 <= at + step < strips
                for source in range(at * rows, (at + 1) * rows):
                    entry += [two[to, source], one[to, source]] if inside else [0.0, 0.0]
        table.append(entry)
    return np.asarray(table, np.float32)


def y_matrices(n):
    grad = np.zeros((n, n))
    div = np.zeros((n, n))
    for k, c in enumerate(coeffs, 1):
        for j in range(n - 1):
            if j + k < n:
                grad[j + k, j] += c
            if j + 1 - k >= 0:
                grad[j + 1 - k, j] -= c
        for i in range(n):
            if i + k - 1 <= n - 2:
                div[i + k - 1, i] += c
            if i - k >= 0:
                div[i - k, i] -= c
    one, two = two_level(n // 2)
    two[1::2] = one[1::2]
    lift = np.zeros((n, n))
    lift[0::2, : n // 2] = one.T
    lift[0::2, n // 2 :] = two.T
    return grad.astype(np.float32), div.astype(np.float32), lift.astype(np.float32)


def z_matrix(n):
    w = np.eye(n)
    for level in range(4):
        w[:: 2**level] = lift_rows(w[:: 2**level])
    return w.astype(np.float32)


def kernel(
    strips, slabs, used,
    cur, prev, stiff, buoy, weights, gy, dy, ly, wz,
    next_out, coef_out,
    cp, bp, fx, acc, pv, sv, nf, gv, dv, lv, wv, con, up, down, up2, down2, zfull, tab,
    lsem, ssem, rsem, zssem, zrsem, gssem, grsem,
):
    p, g = lax.axis_index("xy"), lax.axis_index("gz")
    X, Z, Y = cur.shape
    NC = Z // CHUNK
    HX, HC = X // 2, CHUNK // 2
    part = HX // slabs
    has_l, has_r = p > 0, p < strips - 1
    has_ll, has_rr = p > 1, p < strips - 2
    has_b, has_t = g > 0, g < slabs - 1
    near = ((has_l, p - 1), (has_r, p + 1), (has_ll, p - 2), (has_rr, p + 2))

    def local(src, dst, k):
        return pltpu.make_async_copy(src, dst, lsem.at[k])

    body = pl.ds(HALO, Z)
    loads = [
        local(cur, cp.at[pl.ds(3, X), body], 0),
        local(buoy, bp.at[pl.ds(0, X), body], 1),
        local(gy, gv, 2),
        local(dy, dv, 3),
        local(prev, pv, 4),
        local(stiff, sv, 5),
        local(ly, lv, 6),
        local(wz, wv, 7),
        local(weights, tab, 8 + 2 * NC),
    ]
    for c in loads:
        c.start()

    barrier = pltpu.get_barrier_semaphore()
    for there, q in near:
        @pl.when(there)
        def _():
            pl.semaphore_signal(barrier, inc=1, device_id=(q, g), device_id_type=pl.DeviceIdType.MESH)
    for o in range(1, slabs):
        pl.semaphore_signal(
            barrier, inc=1, device_id=(p, lax.rem(g + o, slabs)), device_id_type=pl.DeviceIdType.MESH
        )

    def zero(ref):
        ref[...] = jnp.zeros(ref.shape, jnp.float32)

    @pl.when(jnp.logical_not(has_l))
    def _():
        zero(cp.at[pl.ds(0, 3), body])
        zero(fx.at[pl.ds(0, 4)])
        zero(up)

    @pl.when(jnp.logical_not(has_r))
    def _():
        zero(cp.at[pl.ds(X + 3, 4), body])
        zero(fx.at[pl.ds(X + 4, 3)])
        zero(down)

    @pl.when(jnp.logical_not(has_ll))
    def _():
        zero(up2)

    @pl.when(jnp.logical_not(has_rr))
    def _():
        zero(down2)

    @pl.when(jnp.logical_not(has_b))
    def _():
        zero(cp.at[pl.ds(3, X), pl.ds(0, HALO)])

    @pl.when(jnp.logical_not(has_t))
    def _():
        zero(cp.at[pl.ds(3, X), pl.ds(HALO + Z, HALO)])

    one = lambda there: there.astype(jnp.int32)
    pl.semaphore_wait(barrier, one(has_l) + one(has_r) + one(has_ll) + one(has_rr) + slabs - 1)

    def remote(src, dst, ss, rs, dev):
        return pltpu.make_async_remote_copy(
            src_ref=src, dst_ref=dst, send_sem=ss, recv_sem=rs, device_id=dev,
            device_id_type=pl.DeviceIdType.MESH,
        )

    def x_copy(kind, c):
        z = pl.ds(c * CHUNK, CHUNK)
        zp = pl.ds(HALO + c * CHUNK, CHUNK)
        sends, q, receives, src, dst = (
            (has_l, p - 1, has_r, cur.at[pl.ds(0, 4), z], cp.at[pl.ds(X + 3, 4), zp]),
            (has_r, p + 1, has_l, cur.at[pl.ds(X - 3, 3), z], cp.at[pl.ds(0, 3), zp]),
            (has_l, p - 1, has_r, buoy.at[pl.ds(0, 1), z], bp.at[pl.ds(X, 1), zp]),
            (has_r, p + 1, has_l, fx.at[pl.ds(X, 4), z], fx.at[pl.ds(0, 4), z]),
            (has_l, p - 1, has_r, fx.at[pl.ds(4, 3), z], fx.at[pl.ds(X + 4, 3), z]),
            (has_r, p + 1, has_l, con.at[c, pl.ds(HX, 4)], up.at[c]),
            (has_l, p - 1, has_r, con.at[c, pl.ds(HX + 4, 5)], down.at[c]),
            (has_rr, p + 2, has_ll, con.at[c, pl.ds(HX + 9, 1)], up2.at[c]),
            (has_ll, p - 2, has_rr, con.at[c, pl.ds(HX + 10, 1)], down2.at[c]),
        )[kind]
        return sends, receives, remote(src, dst, ssem.at[kind, c], rsem.at[kind, c], (q, g))

    def z_copy(kind):
        low, high = pl.ds(0, HALO), pl.ds(Z - HALO, HALO)
        below, above = pl.ds(0, HALO), pl.ds(HALO + Z, HALO)
        sends, q, receives, src, dst = (
            (has_b, g - 1, has_t, cur.at[:, low], cp.at[pl.ds(3, X), above]),
            (has_t, g + 1, has_b, cur.at[:, high], cp.at[pl.ds(3, X), below]),
            (has_b, g - 1, has_t, buoy.at[:, low], bp.at[pl.ds(0, X), above]),
            (has_t, g + 1, has_b, buoy.at[:, high], bp.at[pl.ds(0, X), below]),
        )[kind]
        return sends, receives, remote(src, dst, zssem.at[kind], zrsem.at[kind], (p, q))

    def start(copy):
        sends, _, c = copy
        pl.when(sends)(c.start)

    def arrive(copy):
        _, receives, c = copy
        pl.when(receives)(c.wait_recv)

    def sent(copy):
        sends, _, c = copy
        pl.when(sends)(c.wait_send)

    order = tuple(range(1, NC - 1)) + (0, NC - 1)

    def halo(n):
        if n < NC:
            for kind in (0, 1, 2):
                start(x_copy(kind, order[n]))

    halo(0)
    for kind in range(4):
        start(z_copy(kind))
    halo(1)

    for c in loads[:4]:
        c.wait()

    rows = 4

    def y_part(i, _):
        x = i * rows
        v = cp[pl.ds(x + 3, rows), HALO : HALO + Z, :].reshape(rows * Z, Y)
        b = bp[pl.ds(x, rows), HALO : HALO + Z, :].reshape(rows * Z, Y)
        grad = jnp.dot(v, gv[...], precision=HIGHEST, preferred_element_type=jnp.float32)
        flux = 0.5 * (b + pltpu.roll(b, Y - 1, 1)) * grad
        acc[pl.ds(x, rows)] = jnp.dot(
            flux, dv[...], precision=HIGHEST, preferred_element_type=jnp.float32
        ).reshape(rows, Z, Y)
        return 0

    def z_part(begin, end, first, last):
        n = last - first
        face = lax.broadcasted_iota(jnp.int32, (n, Y), 0) + (first - HALO) + g * Z
        inside = jnp.logical_and(face >= 0, face <= slabs * Z - 2)

        def moved(v, k):
            return pltpu.roll(v, (-k) % n, 0) if k else v

        def row(x, _):
            v, b = cp[x + 3, first:last, :], bp[x, first:last, :]
            grad = None
            for k, w in enumerate(coeffs, 1):
                term = w * (moved(v, k) - moved(v, 1 - k))
                grad = term if grad is None else grad + term
            flux = jnp.where(inside, 0.5 * (b + moved(b, 1)) * grad, 0.0)
            div = None
            for k, w in enumerate(coeffs, 1):
                term = w * (moved(flux, k - 1) - moved(flux, -k))
                div = term if div is None else div + term
            at = begin + HALO - first
            acc[x, begin:end, :] = acc[x, begin:end, :] + div[at : at + end - begin]
            return 0

        lax.fori_loop(0, X, row, 0)

    def flux_part(c):
        for kind in (0, 1, 2):
            arrive(x_copy(kind, c))
        zp = slice(HALO + c * CHUNK, HALO + (c + 1) * CHUNK)
        z = slice(c * CHUNK, (c + 1) * CHUNK)

        def x_flux(x, _):
            grad = None
            for k, w in enumerate(coeffs, 1):
                term = w * (cp[x + 3 + k, zp, :] - cp[x + 4 - k, zp, :])
                grad = term if grad is None else grad + term
            flux = 0.5 * (bp[x, zp, :] + bp[x + 1, zp, :]) * grad
            keep = jnp.logical_or(has_r, x < X - 1)
            fx[x + 4, z, :] = jnp.where(keep, flux, 0.0)
            return 0

        lax.fori_loop(0, X, x_flux, 0)
        start(x_copy(3, c))
        start(x_copy(4, c))

    even = lax.rem(lax.broadcasted_iota(jnp.int32, (HC, Y // 2), 1), 2) == 0
    kind_of = jnp.minimum(p, 2) + jnp.maximum(p - (strips - 3), 0)
    sent_rows = tuple(range(HX)) + UP_ROWS + DOWN_ROWS + UP2_ROWS + DOWN2_ROWS
    stores = []

    def finish_part(c):
        arrive(x_copy(3, c))
        arrive(x_copy(4, c))
        zp = slice(HALO + c * CHUNK, HALO + (c + 1) * CHUNK)
        z = slice(c * CHUNK, (c + 1) * CHUNK)

        def finish(x, _):
            div = None
            for k, w in enumerate(coeffs, 1):
                term = w * (fx[x + 3 + k, z, :] - fx[x + 4 - k, z, :])
                div = term if div is None else div + term
            value = 2.0 * cp[x + 3, zp, :] - pv[x, z, :] + sv[x, z, :] * (div + acc[x, z, :])
            for h in range(Y // 128):
                nf[h, x, z, :] = value[:, h * 128 : (h + 1) * 128]
            return 0

        lax.fori_loop(0, X, finish, 0)
        for h in range(Y // 128):
            zc = pl.ds(c * CHUNK, CHUNK)
            copy = local(nf.at[h, :, zc], next_out.at[:, zc, pl.ds(h * 128, 128)], 8 + 2 * c + h)
            copy.start()
            stores.append(copy)
        snap = jnp.concatenate(
            [
                jnp.concatenate(
                    [nf[h, 2 * r, pl.ds(c * CHUNK, HC, stride=2), :] for h in range(Y // 128)], axis=1
                )
                for r in range(HX)
            ],
            axis=0,
        )
        t = jnp.dot(snap, lv[...], precision=HIGHEST, preferred_element_type=jnp.float32)
        one_y = [t[r * HC : (r + 1) * HC, : Y // 2] for r in range(HX)]
        two_y = [t[r * HC : (r + 1) * HC, Y // 2 :] for r in range(HX)]
        at = 0
        for slot, group in enumerate(sent_rows):
            totals = []
            for row in group if isinstance(group, tuple) else (group,):
                total = None
                for r in range(HX):
                    i = at * HX + r
                    if not used[i]:
                        continue
                    w2, w1 = tab[kind_of, 2 * i], tab[kind_of, 2 * i + 1]
                    term = jnp.where(even, w2, w1) * two_y[r] if row % 2 == 0 else w1 * one_y[r]
                    total = term if total is None else total + term
                totals.append(total)
                at += 1
            con[c, slot] = totals[0] if len(totals) == 1 else totals[0] + pltpu.roll(totals[1], 1, 1)
        for kind in (5, 6, 7, 8):
            start(x_copy(kind, c))

    def g_copy(o, c):
        to = lax.rem(g + o, slabs)
        mine = pl.ds(pl.multiple_of(g * (Z // 2) + c * HC, HC), HC)
        return remote(
            con.at[c, pl.ds(to * part, part)], zfull.at[:, mine],
            gssem.at[o - 1, c], grsem.at[o - 1, c], (p, to),
        )

    def planar_part(c):
        for kind in (5, 6, 7, 8):
            arrive(x_copy(kind, c))
        total = [con[c, row] for row in range(HX)]
        for ref, wanted in ((up, UP_ROWS), (down, DOWN_ROWS), (up2, UP2_ROWS), (down2, DOWN2_ROWS)):
            for slot, group in enumerate(wanted):
                got = ref[c, slot]
                if isinstance(group, tuple):
                    total[group[0]] += jnp.where(even, got, 0.0)
                    total[group[1]] += jnp.where(even, pltpu.roll(got, Y // 2 - 1, 1), 0.0)
                else:
                    total[group] += got
        for row in range(HX):
            con[c, row] = total[row]
        for o in range(1, slabs):
            g_copy(o, c).start()
        zfull[:, pl.ds(pl.multiple_of(g * (Z // 2) + c * HC, HC), HC), :] = con[c, pl.ds(g * part, part)]

    blocks = X // rows
    lax.fori_loop(0, blocks // 2, y_part, 0)
    flux_part(order[0])
    halo(2)
    lax.fori_loop(blocks // 2, blocks, y_part, 0)
    flux_part(order[1])
    halo(3)
    z_part(HALO, Z - HALO, HALO, HALO + Z)
    for c in loads[4:7] + loads[8:]:
        c.wait()
    finish_part(order[0])
    flux_part(order[2])
    finish_part(order[1])
    flux_part(order[3])
    for kind in range(4):
        arrive(z_copy(kind))
    z_part(0, HALO, 0, 3 * HALO)
    z_part(Z - HALO, Z, Z - HALO, Z + 2 * HALO)
    finish_part(order[2])
    planar_part(order[0])
    finish_part(order[3])
    planar_part(order[1])
    planar_part(order[2])
    planar_part(order[3])

    loads[7].wait()
    for c in range(NC):
        for o in range(1, slabs):
            g_copy(o, c).wait_recv()
    for row in range(part):
        coef_out[row] = jnp.dot(
            wv[...], zfull[row], precision=HIGHEST, preferred_element_type=jnp.float32
        )

    for copy in stores:
        copy.wait()
    for kind in range(4):
        sent(z_copy(kind))
    for c in range(NC):
        for kind in range(9):
            sent(x_copy(kind, c))
        for o in range(1, slabs):
            g_copy(o, c).wait_send()


def pin(array):
    return pltpu.with_memory_space_constraint(jnp.asarray(array), pltpu.HBM)


def on_device(strips, slabs, previous, current, stiffness, buoyancy):
    X, Z, Y = current.shape
    NC, HX, HC = Z // CHUNK, X // 2, CHUNK // 2
    depth = slabs * Z // 2
    grad, div, lift = y_matrices(Y)
    hbm = pl.BlockSpec(memory_space=pltpu.HBM)
    table = x_table(strips, HX)
    used = tuple((table != 0).any(0).reshape(-1, 2).any(1).tolist())
    f32 = jnp.float32
    vmem = lambda *shape: pltpu.VMEM(shape, f32)
    dma = lambda *shape: pltpu.SemaphoreType.DMA(shape)
    return pl.pallas_call(
        functools.partial(kernel, strips, slabs, used),
        out_shape=(
            jax.ShapeDtypeStruct((X, Z, Y), f32),
            jax.ShapeDtypeStruct((HX // slabs, depth, Y // 2), f32),
        ),
        in_specs=[hbm] * 9,
        out_specs=(hbm, pl.BlockSpec(memory_space=pltpu.VMEM)),
        scratch_shapes=[
            vmem(X + 7, Z + 2 * HALO, Y),
            vmem(X + 1, Z + 2 * HALO, Y),
            vmem(X + 7, Z, Y),
            vmem(X, Z, Y),
            vmem(X, Z, Y),
            vmem(X, Z, Y),
            vmem(Y // 128, X, Z, 128),
            vmem(Y, Y),
            vmem(Y, Y),
            vmem(Y, Y),
            vmem(depth, depth),
            vmem(NC, HX + 11, HC, Y // 2),
            vmem(NC, 4, HC, Y // 2),
            vmem(NC, 5, HC, Y // 2),
            vmem(NC, 1, HC, Y // 2),
            vmem(NC, 1, HC, Y // 2),
            vmem(HX // slabs, depth, Y // 2),
            pltpu.SMEM(table.shape, f32),
            dma(9 + 2 * NC),
            dma(9, NC),
            dma(9, NC),
            dma(4),
            dma(4),
            dma(slabs - 1, NC),
            dma(slabs - 1, NC),
        ],
        compiler_params=pltpu.CompilerParams(
            collective_id=0, has_side_effects=True, vmem_limit_bytes=40 * 1024 * 1024
        ),
    )(
        pin(current), pin(previous), pin(stiffness), pin(buoyancy),
        pin(table), pin(grad), pin(div), pin(lift), pin(z_matrix(depth)),
    )


def solution(mesh):
    return jax.shard_map(
        functools.partial(on_device, mesh.shape["xy"], mesh.shape["gz"]),
        mesh=mesh,
        in_specs=(P("xy", "gz", None),) * 4,
        out_specs=(P("xy", "gz", None), P(("xy", "gz"), None, None)),
        check_vma=False,
    )
```

```python
import functools

import jax
import jax.numpy as jnp
import numpy as np
from jax import lax
from jax.experimental import pallas as pl
from jax.experimental.pallas import tpu as pltpu
from jax.sharding import PartitionSpec as P

coeffs = (1225.0 / 1024.0, -245.0 / 3072.0, 49.0 / 5120.0, -5.0 / 7168.0)
alpha_lift = -1.586134342
beta_lift = -0.05298011854
gamma_lift = 0.8829110762
delta_lift = 0.4435068522
wavelet_scale = 1.149604398

FLOWS = (
    (0, (0, 1, 2, 3, 4, 5, 6, 7)),
    (1, (0, 1, 2, (4, 6))),
    (-1, (4, 5, 6, 7, (0, 2))),
    (2, (0,)),
    (-2, ((4, 6),)),
)
SLOTS = tuple(slot for _, slots in FLOWS for slot in slots)
CHUNK = 16
HALO = 8
HIGHEST = lax.Precision.HIGHEST


def lift_rows(v):
    s, d = v[0::2].copy(), v[1::2].copy()
    nxt = lambda a: np.concatenate([a[1:], a[-1:]])
    prv = lambda a: np.concatenate([a[:1], a[:-1]])
    d = d + alpha_lift * (s + nxt(s))
    s = s + beta_lift * (prv(d) + d)
    d = d + gamma_lift * (s + nxt(s))
    s = s + delta_lift * (prv(d) + d)
    out = np.empty_like(v)
    out[0::2], out[1::2] = s * wavelet_scale, d / wavelet_scale
    return out


def two_level(n):
    one = lift_rows(np.eye(n))
    two = one.copy()
    two[0::2] = lift_rows(one[0::2])
    return one, two


def pair(slot):
    return slot if isinstance(slot, tuple) else (slot,)


def owned(slots, owner, part):
    mine = [i for i, slot in enumerate(slots) if any(row // part == owner for row in pair(slot))]
    assert mine == list(range(mine[0], mine[0] + len(mine))) if mine else True
    return (mine[0], len(mine)) if mine else (0, 0)


def x_table(strips, rows):
    one, two = two_level(strips * rows)
    table = []
    for at in (0, 1, 2, strips - 2, strips - 1):
        entry = []
        for step, slots in FLOWS:
            for row in (row for slot in slots for row in pair(slot)):
                to = (at + step) * rows + row
                inside = 0 <= at + step < strips
                for source in range(at * rows, (at + 1) * rows):
                    entry += [two[to, source], one[to, source]] if inside else [0.0, 0.0]
        table.append(entry)
    return np.asarray(table, np.float32)


def y_matrices(n):
    grad = np.zeros((n, n))
    div = np.zeros((n, n))
    for k, c in enumerate(coeffs, 1):
        for j in range(n - 1):
            if j + k < n:
                grad[j + k, j] += c
            if j + 1 - k >= 0:
                grad[j + 1 - k, j] -= c
        for i in range(n):
            if i + k - 1 <= n - 2:
                div[i + k - 1, i] += c
            if i - k >= 0:
                div[i - k, i] -= c
    one, two = two_level(n // 2)
    two[1::2] = one[1::2]
    lift = np.zeros((n, n))
    lift[0::2, : n // 2] = one.T
    lift[0::2, n // 2 :] = two.T
    return grad.astype(np.float32), div.astype(np.float32), lift.astype(np.float32)


def z_matrix(n):
    w = np.eye(n)
    for level in range(4):
        w[:: 2**level] = lift_rows(w[:: 2**level])
    return w.astype(np.float32)


def kernel(
    strips, slabs, used,
    cur, prev, stiff, buoy, weights, gy, dy, ly, wz,
    next_out, coef_out,
    cp, bp, fx, acc, pv, sv, nf, gv, dv, lv, wv, con, got, zfull, tab,
    lsem, ssem, rsem, zssem, zrsem, cssem, crsem,
):
    p, g = lax.axis_index("xy"), lax.axis_index("gz")
    X, Z, Y = cur.shape
    NC = Z // CHUNK
    HX, HC = X // 2, CHUNK // 2
    part = HX // slabs
    has_l, has_r = p > 0, p < strips - 1
    has_ll, has_rr = p > 1, p < strips - 2
    has_b, has_t = g > 0, g < slabs - 1
    near = ((has_l, p - 1), (has_r, p + 1), (has_ll, p - 2), (has_rr, p + 2))
    reach = {0: True, 1: has_r, -1: has_l, 2: has_rr, -2: has_ll}

    def local(src, dst, k):
        return pltpu.make_async_copy(src, dst, lsem.at[k])

    body = pl.ds(HALO, Z)
    loads = [
        local(cur, cp.at[pl.ds(3, X), body], 0),
        local(buoy, bp.at[pl.ds(0, X), body], 1),
        local(gy, gv, 2),
        local(dy, dv, 3),
        local(prev, pv, 4),
        local(stiff, sv, 5),
        local(ly, lv, 6),
        local(wz, wv, 7),
        local(weights, tab, 8 + 2 * NC),
    ]
    for c in loads:
        c.start()

    barrier = pltpu.get_barrier_semaphore()
    for there, q in near:
        @pl.when(there)
        def _():
            for o in range(slabs):
                pl.semaphore_signal(barrier, inc=1, device_id=(q, o), device_id_type=pl.DeviceIdType.MESH)
    for o in range(1, slabs):
        pl.semaphore_signal(
            barrier, inc=1, device_id=(p, lax.rem(g + o, slabs)), device_id_type=pl.DeviceIdType.MESH
        )

    room, base = [], []
    for _, slots in FLOWS:
        base.append(sum(room))
        room.append(max(owned(slots, o, part)[1] for o in range(slabs)))

    def zero(ref):
        ref[...] = jnp.zeros(ref.shape, jnp.float32)

    @pl.when(jnp.logical_not(has_l))
    def _():
        zero(cp.at[pl.ds(0, 3), body])
        zero(fx.at[pl.ds(0, 4)])
        zero(got.at[:, :, pl.ds(base[1], room[1])])

    @pl.when(jnp.logical_not(has_r))
    def _():
        zero(cp.at[pl.ds(X + 3, 4), body])
        zero(fx.at[pl.ds(X + 4, 3)])
        zero(got.at[:, :, pl.ds(base[2], room[2])])

    @pl.when(jnp.logical_not(has_ll))
    def _():
        zero(got.at[:, :, pl.ds(base[3], room[3])])

    @pl.when(jnp.logical_not(has_rr))
    def _():
        zero(got.at[:, :, pl.ds(base[4], room[4])])

    @pl.when(jnp.logical_not(has_b))
    def _():
        zero(cp.at[pl.ds(3, X), pl.ds(0, HALO)])

    @pl.when(jnp.logical_not(has_t))
    def _():
        zero(cp.at[pl.ds(3, X), pl.ds(HALO + Z, HALO)])

    one = lambda there: there.astype(jnp.int32)
    pl.semaphore_wait(barrier, slabs * (one(has_l) + one(has_r) + one(has_ll) + one(has_rr)) + slabs - 1)

    def remote(src, dst, ss, rs, dev):
        return pltpu.make_async_remote_copy(
            src_ref=src, dst_ref=dst, send_sem=ss, recv_sem=rs, device_id=dev,
            device_id_type=pl.DeviceIdType.MESH,
        )

    def x_copy(kind, c):
        z = pl.ds(c * CHUNK, CHUNK)
        zp = pl.ds(HALO + c * CHUNK, CHUNK)
        sends, q, receives, src, dst = (
            (has_l, p - 1, has_r, cur.at[pl.ds(0, 4), z], cp.at[pl.ds(X + 3, 4), zp]),
            (has_r, p + 1, has_l, cur.at[pl.ds(X - 3, 3), z], cp.at[pl.ds(0, 3), zp]),
            (has_l, p - 1, has_r, buoy.at[pl.ds(0, 1), z], bp.at[pl.ds(X, 1), zp]),
            (has_r, p + 1, has_l, fx.at[pl.ds(X, 4), z], fx.at[pl.ds(0, 4), z]),
            (has_l, p - 1, has_r, fx.at[pl.ds(4, 3), z], fx.at[pl.ds(X + 4, 3), z]),
        )[kind]
        return sends, receives, remote(src, dst, ssem.at[kind, c], rsem.at[kind, c], (q, g))

    def z_copy(kind):
        low, high = pl.ds(0, HALO), pl.ds(Z - HALO, HALO)
        below, above = pl.ds(0, HALO), pl.ds(HALO + Z, HALO)
        sends, q, receives, src, dst = (
            (has_b, g - 1, has_t, cur.at[:, low], cp.at[pl.ds(3, X), above]),
            (has_t, g + 1, has_b, cur.at[:, high], cp.at[pl.ds(3, X), below]),
            (has_b, g - 1, has_t, buoy.at[:, low], bp.at[pl.ds(0, X), above]),
            (has_t, g + 1, has_b, buoy.at[:, high], bp.at[pl.ds(0, X), below]),
        )[kind]
        return sends, receives, remote(src, dst, zssem.at[kind], zrsem.at[kind], (p, q))

    def start(copy):
        if copy is None:
            return
        sends, _, c = copy
        pl.when(sends)(c.start)

    def arrive(copy):
        if copy is None:
            return
        _, receives, c = copy
        pl.when(receives)(c.wait_recv)

    def sent(copy):
        if copy is None:
            return
        sends, _, c = copy
        pl.when(sends)(c.wait_send)

    order = tuple(range(1, NC - 1)) + (0, NC - 1)

    def halo(n):
        if n < NC:
            for kind in (0, 1, 2):
                start(x_copy(kind, order[n]))

    halo(0)
    for kind in range(4):
        start(z_copy(kind))
    halo(1)

    for c in loads[:4]:
        c.wait()

    rows = 4

    def y_part(i, _):
        x = i * rows
        v = cp[pl.ds(x + 3, rows), HALO : HALO + Z, :].reshape(rows * Z, Y)
        b = bp[pl.ds(x, rows), HALO : HALO + Z, :].reshape(rows * Z, Y)
        grad = jnp.dot(v, gv[...], precision=HIGHEST, preferred_element_type=jnp.float32)
        flux = 0.5 * (b + pltpu.roll(b, Y - 1, 1)) * grad
        acc[pl.ds(x, rows)] = jnp.dot(
            flux, dv[...], precision=HIGHEST, preferred_element_type=jnp.float32
        ).reshape(rows, Z, Y)
        return 0

    def z_part(begin, end, first, last):
        n = last - first
        face = lax.broadcasted_iota(jnp.int32, (n, Y), 0) + (first - HALO) + g * Z
        inside = jnp.logical_and(face >= 0, face <= slabs * Z - 2)

        def moved(v, k):
            return pltpu.roll(v, (-k) % n, 0) if k else v

        def row(x, _):
            v, b = cp[x + 3, first:last, :], bp[x, first:last, :]
            grad = None
            for k, w in enumerate(coeffs, 1):
                term = w * (moved(v, k) - moved(v, 1 - k))
                grad = term if grad is None else grad + term
            flux = jnp.where(inside, 0.5 * (b + moved(b, 1)) * grad, 0.0)
            div = None
            for k, w in enumerate(coeffs, 1):
                term = w * (moved(flux, k - 1) - moved(flux, -k))
                div = term if div is None else div + term
            at = begin + HALO - first
            acc[x, begin:end, :] = acc[x, begin:end, :] + div[at : at + end - begin]
            return 0

        lax.fori_loop(0, X, row, 0)

    def flux_part(c):
        for kind in (0, 1, 2):
            arrive(x_copy(kind, c))
        zp = slice(HALO + c * CHUNK, HALO + (c + 1) * CHUNK)
        z = slice(c * CHUNK, (c + 1) * CHUNK)

        def x_flux(x, _):
            grad = None
            for k, w in enumerate(coeffs, 1):
                term = w * (cp[x + 3 + k, zp, :] - cp[x + 4 - k, zp, :])
                grad = term if grad is None else grad + term
            flux = 0.5 * (bp[x, zp, :] + bp[x + 1, zp, :]) * grad
            keep = jnp.logical_or(has_r, x < X - 1)
            fx[x + 4, z, :] = jnp.where(keep, flux, 0.0)
            return 0

        lax.fori_loop(0, X, x_flux, 0)
        start(x_copy(3, c))
        start(x_copy(4, c))

    even = lax.rem(lax.broadcasted_iota(jnp.int32, (HC, Y // 2), 1), 2) == 0
    kind_of = jnp.minimum(p, 2) + jnp.maximum(p - (strips - 3), 0)
    stores = []

    def finish_part(c):
        arrive(x_copy(3, c))
        arrive(x_copy(4, c))
        zp = slice(HALO + c * CHUNK, HALO + (c + 1) * CHUNK)
        z = slice(c * CHUNK, (c + 1) * CHUNK)

        def finish(x, _):
            div = None
            for k, w in enumerate(coeffs, 1):
                term = w * (fx[x + 3 + k, z, :] - fx[x + 4 - k, z, :])
                div = term if div is None else div + term
            value = 2.0 * cp[x + 3, zp, :] - pv[x, z, :] + sv[x, z, :] * (div + acc[x, z, :])
            for h in range(Y // 128):
                nf[h, x, z, :] = value[:, h * 128 : (h + 1) * 128]
            return 0

        lax.fori_loop(0, X, finish, 0)
        for h in range(Y // 128):
            zc = pl.ds(c * CHUNK, CHUNK)
            copy = local(nf.at[h, :, zc], next_out.at[:, zc, pl.ds(h * 128, 128)], 8 + 2 * c + h)
            copy.start()
            stores.append(copy)
        snap = jnp.concatenate(
            [
                jnp.concatenate(
                    [nf[h, 2 * r, pl.ds(c * CHUNK, HC, stride=2), :] for h in range(Y // 128)], axis=1
                )
                for r in range(HX)
            ],
            axis=0,
        )
        t = jnp.dot(snap, lv[...], precision=HIGHEST, preferred_element_type=jnp.float32)
        one_y = [t[r * HC : (r + 1) * HC, : Y // 2] for r in range(HX)]
        two_y = [t[r * HC : (r + 1) * HC, Y // 2 :] for r in range(HX)]
        at = 0
        for slot, group in enumerate(SLOTS):
            totals = []
            for row in pair(group):
                total = None
                for r in range(HX):
                    i = at * HX + r
                    if not used[i]:
                        continue
                    w2, w1 = tab[kind_of, 2 * i], tab[kind_of, 2 * i + 1]
                    term = jnp.where(even, w2, w1) * two_y[r] if row % 2 == 0 else w1 * one_y[r]
                    total = term if total is None else total + term
                totals.append(total)
                at += 1
            con[c, slot] = totals[0] if len(totals) == 1 else totals[0] + pltpu.roll(totals[1], 1, 1)
        for f in range(len(FLOWS)):
            for o in range(slabs):
                start(sum_copy(f, o, None, c))
        for o in range(slabs):
            @pl.when(g == o)
            def _():
                first, n = owned(FLOWS[0][1], o, part)
                got[c, o, 0:n] = con[c, first : first + n]

    def sum_copy(f, o, s, c):
        step, slots = FLOWS[f]
        first, n = owned(slots, o, part)
        if not n:
            return None
        here = sum(len(slots) for _, slots in FLOWS[:f]) + first
        copy = remote(
            con.at[c, pl.ds(here, n)], got.at[c, g if s is None else s, pl.ds(base[f], n)],
            cssem.at[f, o, c], crsem.at[f, g if s is None else s, c], (p + step, o),
        )
        return (reach[step] if step else g != o), (reach[-step] if step else g != s), copy

    def planar_part(c):
        for o in range(slabs):
            @pl.when(g == o)
            def _():
                for s in range(slabs):
                    total = [None] * part
                    for f, (_, slots) in enumerate(FLOWS):
                        arrive(sum_copy(f, o, s, c))
                    for f, (_, slots) in enumerate(FLOWS):
                        first, n = owned(slots, o, part)
                        for i in range(n):
                            slot = slots[first + i]
                            value = got[c, s, base[f] + i]
                            for at, row in enumerate(pair(slot)):
                                if row // part != o:
                                    continue
                                term = value
                                if isinstance(slot, tuple):
                                    term = pltpu.roll(value, Y // 2 - 1, 1) if at else value
                                    term = jnp.where(even, term, 0.0)
                                k = row - o * part
                                total[k] = term if total[k] is None else total[k] + term
                    at = s * (Z // 2) + c * HC
                    for k in range(part):
                        zfull[k, at : at + HC, :] = total[k]

    blocks = X // rows
    lax.fori_loop(0, blocks // 2, y_part, 0)
    flux_part(order[0])
    halo(2)
    lax.fori_loop(blocks // 2, blocks, y_part, 0)
    flux_part(order[1])
    halo(3)
    z_part(HALO, Z - HALO, HALO, HALO + Z)
    flux_part(order[2])
    for c in loads[4:7] + loads[8:]:
        c.wait()
    finish_part(order[0])
    flux_part(order[3])
    finish_part(order[1])
    for kind in range(4):
        arrive(z_copy(kind))
    z_part(0, HALO, 0, 3 * HALO)
    z_part(Z - HALO, Z, Z - HALO, Z + 2 * HALO)
    finish_part(order[2])
    planar_part(order[0])
    finish_part(order[3])
    loads[7].wait()
    for n in range(1, NC):
        planar_part(order[n])
    for row in range(part):
        coef_out[row] = jnp.dot(
            wv[...], zfull[row], precision=HIGHEST, preferred_element_type=jnp.float32
        )

    for copy in stores:
        copy.wait()
    for kind in range(4):
        sent(z_copy(kind))
    for c in range(NC):
        for kind in range(5):
            sent(x_copy(kind, c))
        for f in range(len(FLOWS)):
            for o in range(slabs):
                sent(sum_copy(f, o, None, c))


def pin(array):
    return pltpu.with_memory_space_constraint(jnp.asarray(array), pltpu.HBM)


def on_device(strips, slabs, previous, current, stiffness, buoyancy):
    X, Z, Y = current.shape
    NC, HX, HC = Z // CHUNK, X // 2, CHUNK // 2
    depth = slabs * Z // 2
    grad, div, lift = y_matrices(Y)
    hbm = pl.BlockSpec(memory_space=pltpu.HBM)
    part = HX // slabs
    places = sum(max(owned(slots, o, part)[1] for o in range(slabs)) for _, slots in FLOWS)
    table = x_table(strips, HX)
    used = tuple((table != 0).any(0).reshape(-1, 2).any(1).tolist())
    f32 = jnp.float32
    vmem = lambda *shape: pltpu.VMEM(shape, f32)
    dma = lambda *shape: pltpu.SemaphoreType.DMA(shape)
    return pl.pallas_call(
        functools.partial(kernel, strips, slabs, used),
        out_shape=(
            jax.ShapeDtypeStruct((X, Z, Y), f32),
            jax.ShapeDtypeStruct((HX // slabs, depth, Y // 2), f32),
        ),
        in_specs=[hbm] * 9,
        out_specs=(hbm, pl.BlockSpec(memory_space=pltpu.VMEM)),
        scratch_shapes=[
            vmem(X + 7, Z + 2 * HALO, Y),
            vmem(X + 1, Z + 2 * HALO, Y),
            vmem(X + 7, Z, Y),
            vmem(X, Z, Y),
            vmem(X, Z, Y),
            vmem(X, Z, Y),
            vmem(Y // 128, X, Z, 128),
            vmem(Y, Y),
            vmem(Y, Y),
            vmem(Y, Y),
            vmem(depth, depth),
            vmem(NC, len(SLOTS), HC, Y // 2),
            vmem(NC, slabs, places, HC, Y // 2),
            vmem(HX // slabs, depth, Y // 2),
            pltpu.SMEM(table.shape, f32),
            dma(9 + 2 * NC),
            dma(5, NC),
            dma(5, NC),
            dma(4),
            dma(4),
            dma(len(FLOWS), slabs, NC),
            dma(len(FLOWS), slabs, NC),
        ],
        compiler_params=pltpu.CompilerParams(
            collective_id=0, has_side_effects=True, vmem_limit_bytes=40 * 1024 * 1024
        ),
    )(
        pin(current), pin(previous), pin(stiffness), pin(buoyancy),
        pin(table), pin(grad), pin(div), pin(lift), pin(z_matrix(depth)),
    )


def solution(mesh):
    return jax.shard_map(
        functools.partial(on_device, mesh.shape["xy"], mesh.shape["gz"]),
        mesh=mesh,
        in_specs=(P("xy", "gz", None),) * 4,
        out_specs=(P("xy", "gz", None), P(("xy", "gz"), None, None)),
        check_vma=False,
    )
```

```python
import functools

import jax
import jax.numpy as jnp
import numpy as np
from jax import lax
from jax.experimental import pallas as pl
from jax.experimental.pallas import tpu as pltpu
from jax.sharding import PartitionSpec as P

coeffs = (1225.0 / 1024.0, -245.0 / 3072.0, 49.0 / 5120.0, -5.0 / 7168.0)
alpha_lift = -1.586134342
beta_lift = -0.05298011854
gamma_lift = 0.8829110762
delta_lift = 0.4435068522
wavelet_scale = 1.149604398

FLOWS = (
    (0, (0, 1, 2, 3, 4, 5, 6, 7)),
    (1, (0, 1, 2, (4, 6))),
    (-1, (4, 5, 6, 7, (0, 2))),
    (2, (0,)),
    (-2, ((4, 6),)),
)
SLOTS = tuple(slot for _, slots in FLOWS for slot in slots)
CHUNK = 16
HALO = 8
HIGHEST = lax.Precision.HIGHEST


def lift_rows(v):
    s, d = v[0::2].copy(), v[1::2].copy()
    nxt = lambda a: np.concatenate([a[1:], a[-1:]])
    prv = lambda a: np.concatenate([a[:1], a[:-1]])
    d = d + alpha_lift * (s + nxt(s))
    s = s + beta_lift * (prv(d) + d)
    d = d + gamma_lift * (s + nxt(s))
    s = s + delta_lift * (prv(d) + d)
    out = np.empty_like(v)
    out[0::2], out[1::2] = s * wavelet_scale, d / wavelet_scale
    return out


def two_level(n):
    one = lift_rows(np.eye(n))
    two = one.copy()
    two[0::2] = lift_rows(one[0::2])
    return one, two


def pair(slot):
    return slot if isinstance(slot, tuple) else (slot,)


def owned(slots, owner, part):
    mine = [i for i, slot in enumerate(slots) if any(row // part == owner for row in pair(slot))]
    assert mine == list(range(mine[0], mine[0] + len(mine))) if mine else True
    return (mine[0], len(mine)) if mine else (0, 0)


def x_table(strips, rows):
    one, two = two_level(strips * rows)
    table = []
    for at in (0, 1, 2, strips - 2, strips - 1):
        entry = []
        for step, slots in FLOWS:
            for row in (row for slot in slots for row in pair(slot)):
                to = (at + step) * rows + row
                inside = 0 <= at + step < strips
                for source in range(at * rows, (at + 1) * rows):
                    entry += [two[to, source], one[to, source]] if inside else [0.0, 0.0]
        table.append(entry)
    return np.asarray(table, np.float32)


def y_matrices(n):
    grad = np.zeros((n, n))
    div = np.zeros((n, n))
    for k, c in enumerate(coeffs, 1):
        for j in range(n - 1):
            if j + k < n:
                grad[j + k, j] += c
            if j + 1 - k >= 0:
                grad[j + 1 - k, j] -= c
        for i in range(n):
            if i + k - 1 <= n - 2:
                div[i + k - 1, i] += c
            if i - k >= 0:
                div[i - k, i] -= c
    one, two = two_level(n // 2)
    two[1::2] = one[1::2]
    lift = np.zeros((n, n))
    lift[0::2, : n // 2] = one.T
    lift[0::2, n // 2 :] = two.T
    return grad.astype(np.float32), div.astype(np.float32), lift.astype(np.float32)


def z_matrix(n):
    w = np.eye(n)
    for level in range(4):
        w[:: 2**level] = lift_rows(w[:: 2**level])
    return w.astype(np.float32)


def kernel(
    strips, slabs, used,
    cur, prev, stiff, buoy, weights, gy, dy, ly,
    next_out, zfull,
    cp, bp, fx, acc, pv, sv, nf, gv, dv, lv, con, got, tab,
    lsem, ssem, rsem, zssem, zrsem, cssem, crsem,
):
    p, g = lax.axis_index("xy"), lax.axis_index("gz")
    X, Z, Y = cur.shape
    NC = Z // CHUNK
    HX, HC = X // 2, CHUNK // 2
    part = HX // slabs
    has_l, has_r = p > 0, p < strips - 1
    has_ll, has_rr = p > 1, p < strips - 2
    has_b, has_t = g > 0, g < slabs - 1
    near = ((has_l, p - 1), (has_r, p + 1), (has_ll, p - 2), (has_rr, p + 2))
    reach = {0: True, 1: has_r, -1: has_l, 2: has_rr, -2: has_ll}

    def local(src, dst, k):
        return pltpu.make_async_copy(src, dst, lsem.at[k])

    body = pl.ds(HALO, Z)
    loads = [
        local(cur, cp.at[pl.ds(3, X), body], 0),
        local(buoy, bp.at[pl.ds(0, X), body], 1),
        local(gy, gv, 2),
        local(dy, dv, 3),
        local(prev, pv, 4),
        local(stiff, sv, 5),
        local(ly, lv, 6),
        local(weights, tab, 7),
    ]
    for c in loads:
        c.start()

    barrier = pltpu.get_barrier_semaphore()
    for there, q in near:
        @pl.when(there)
        def _():
            for o in range(slabs):
                pl.semaphore_signal(barrier, inc=1, device_id=(q, o), device_id_type=pl.DeviceIdType.MESH)
    for o in range(1, slabs):
        pl.semaphore_signal(
            barrier, inc=1, device_id=(p, lax.rem(g + o, slabs)), device_id_type=pl.DeviceIdType.MESH
        )

    room, base = [], []
    for _, slots in FLOWS:
        base.append(sum(room))
        room.append(max(owned(slots, o, part)[1] for o in range(slabs)))

    def zero(ref):
        ref[...] = jnp.zeros(ref.shape, jnp.float32)

    @pl.when(jnp.logical_not(has_l))
    def _():
        zero(cp.at[pl.ds(0, 3), body])
        zero(fx.at[pl.ds(0, 4)])
        zero(got.at[:, :, pl.ds(base[1], room[1])])

    @pl.when(jnp.logical_not(has_r))
    def _():
        zero(cp.at[pl.ds(X + 3, 4), body])
        zero(fx.at[pl.ds(X + 4, 3)])
        zero(got.at[:, :, pl.ds(base[2], room[2])])

    @pl.when(jnp.logical_not(has_ll))
    def _():
        zero(got.at[:, :, pl.ds(base[3], room[3])])

    @pl.when(jnp.logical_not(has_rr))
    def _():
        zero(got.at[:, :, pl.ds(base[4], room[4])])

    @pl.when(jnp.logical_not(has_b))
    def _():
        zero(cp.at[pl.ds(3, X), pl.ds(0, HALO)])

    @pl.when(jnp.logical_not(has_t))
    def _():
        zero(cp.at[pl.ds(3, X), pl.ds(HALO + Z, HALO)])

    one = lambda there: there.astype(jnp.int32)
    pl.semaphore_wait(barrier, slabs * (one(has_l) + one(has_r) + one(has_ll) + one(has_rr)) + slabs - 1)

    def remote(src, dst, ss, rs, dev):
        return pltpu.make_async_remote_copy(
            src_ref=src, dst_ref=dst, send_sem=ss, recv_sem=rs, device_id=dev,
            device_id_type=pl.DeviceIdType.MESH,
        )

    def x_copy(kind, c):
        z = pl.ds(c * CHUNK, CHUNK)
        zp = pl.ds(HALO + c * CHUNK, CHUNK)
        sends, q, receives, src, dst = (
            (has_l, p - 1, has_r, cur.at[pl.ds(0, 4), z], cp.at[pl.ds(X + 3, 4), zp]),
            (has_r, p + 1, has_l, cur.at[pl.ds(X - 3, 3), z], cp.at[pl.ds(0, 3), zp]),
            (has_l, p - 1, has_r, buoy.at[pl.ds(0, 1), z], bp.at[pl.ds(X, 1), zp]),
            (has_r, p + 1, has_l, fx.at[pl.ds(X, 4), z], fx.at[pl.ds(0, 4), z]),
            (has_l, p - 1, has_r, fx.at[pl.ds(4, 3), z], fx.at[pl.ds(X + 4, 3), z]),
        )[kind]
        return sends, receives, remote(src, dst, ssem.at[kind, c], rsem.at[kind, c], (q, g))

    def z_copy(kind):
        low, high = pl.ds(0, HALO), pl.ds(Z - HALO, HALO)
        below, above = pl.ds(0, HALO), pl.ds(HALO + Z, HALO)
        sends, q, receives, src, dst = (
            (has_b, g - 1, has_t, cur.at[:, low], cp.at[pl.ds(3, X), above]),
            (has_t, g + 1, has_b, cur.at[:, high], cp.at[pl.ds(3, X), below]),
            (has_b, g - 1, has_t, buoy.at[:, low], bp.at[pl.ds(0, X), above]),
            (has_t, g + 1, has_b, buoy.at[:, high], bp.at[pl.ds(0, X), below]),
        )[kind]
        return sends, receives, remote(src, dst, zssem.at[kind], zrsem.at[kind], (p, q))

    def start(copy):
        if copy is None:
            return
        sends, _, c = copy
        pl.when(sends)(c.start)

    def arrive(copy):
        if copy is None:
            return
        _, receives, c = copy
        pl.when(receives)(c.wait_recv)

    def sent(copy):
        if copy is None:
            return
        sends, _, c = copy
        pl.when(sends)(c.wait_send)

    order = tuple(range(1, NC - 1)) + (0, NC - 1)

    def halo(n):
        if n < NC:
            for kind in (0, 1, 2):
                start(x_copy(kind, order[n]))

    for n in range(3):
        halo(n)

    for c in loads[:4]:
        c.wait()

    rows = 4

    def y_part(i, _):
        x = i * rows
        v = cp[pl.ds(x + 3, rows), HALO : HALO + Z, :].reshape(rows * Z, Y)
        b = bp[pl.ds(x, rows), HALO : HALO + Z, :].reshape(rows * Z, Y)
        grad = jnp.dot(v, gv[...], precision=HIGHEST, preferred_element_type=jnp.float32)
        flux = 0.5 * (b + pltpu.roll(b, Y - 1, 1)) * grad
        acc[pl.ds(x, rows)] = jnp.dot(
            flux, dv[...], precision=HIGHEST, preferred_element_type=jnp.float32
        ).reshape(rows, Z, Y)
        return 0

    def z_part(begin, end, first, last):
        n = last - first
        face = lax.broadcasted_iota(jnp.int32, (n, Y), 0) + (first - HALO) + g * Z
        inside = jnp.logical_and(face >= 0, face <= slabs * Z - 2)

        def moved(v, k):
            return pltpu.roll(v, (-k) % n, 0) if k else v

        def row(x, _):
            v, b = cp[x + 3, first:last, :], bp[x, first:last, :]
            grad = None
            for k, w in enumerate(coeffs, 1):
                term = w * (moved(v, k) - moved(v, 1 - k))
                grad = term if grad is None else grad + term
            flux = jnp.where(inside, 0.5 * (b + moved(b, 1)) * grad, 0.0)
            div = None
            for k, w in enumerate(coeffs, 1):
                term = w * (moved(flux, k - 1) - moved(flux, -k))
                div = term if div is None else div + term
            at = begin + HALO - first
            acc[x, begin:end, :] = acc[x, begin:end, :] + div[at : at + end - begin]
            return 0

        lax.fori_loop(0, X, row, 0)

    def flux_part(c):
        for kind in (0, 1, 2):
            arrive(x_copy(kind, c))
        zp = slice(HALO + c * CHUNK, HALO + (c + 1) * CHUNK)
        z = slice(c * CHUNK, (c + 1) * CHUNK)

        def x_flux(x, _):
            grad = None
            for k, w in enumerate(coeffs, 1):
                term = w * (cp[x + 3 + k, zp, :] - cp[x + 4 - k, zp, :])
                grad = term if grad is None else grad + term
            flux = 0.5 * (bp[x, zp, :] + bp[x + 1, zp, :]) * grad
            keep = jnp.logical_or(has_r, x < X - 1)
            fx[x + 4, z, :] = jnp.where(keep, flux, 0.0)
            return 0

        lax.fori_loop(X - 4, X, x_flux, 0)
        start(x_copy(3, c))
        lax.fori_loop(0, 3, x_flux, 0)
        start(x_copy(4, c))
        lax.fori_loop(3, X - 4, x_flux, 0)

    even = lax.rem(lax.broadcasted_iota(jnp.int32, (HC, Y // 2), 1), 2) == 0
    kind_of = jnp.minimum(p, 2) + jnp.maximum(p - (strips - 3), 0)
    stores = []

    def finish_part(c):
        arrive(x_copy(3, c))
        arrive(x_copy(4, c))
        zp = slice(HALO + c * CHUNK, HALO + (c + 1) * CHUNK)
        z = slice(c * CHUNK, (c + 1) * CHUNK)

        def finish(x, _):
            div = None
            for k, w in enumerate(coeffs, 1):
                term = w * (fx[x + 3 + k, z, :] - fx[x + 4 - k, z, :])
                div = term if div is None else div + term
            value = 2.0 * cp[x + 3, zp, :] - pv[x, z, :] + sv[x, z, :] * (div + acc[x, z, :])
            for h in range(Y // 128):
                nf[h, x, z, :] = value[:, h * 128 : (h + 1) * 128]
            return 0

        lax.fori_loop(0, X, finish, 0)
        for h in range(Y // 128):
            zc = pl.ds(c * CHUNK, CHUNK)
            copy = local(nf.at[h, :, zc], next_out.at[:, zc, pl.ds(h * 128, 128)], 8 + 2 * c + h)
            copy.start()
            stores.append(copy)
        snap = jnp.concatenate(
            [
                jnp.concatenate(
                    [nf[h, 2 * r, pl.ds(c * CHUNK, HC, stride=2), :] for h in range(Y // 128)], axis=1
                )
                for r in range(HX)
            ],
            axis=0,
        )
        t = jnp.dot(snap, lv[...], precision=HIGHEST, preferred_element_type=jnp.float32)
        one_y = [t[r * HC : (r + 1) * HC, : Y // 2] for r in range(HX)]
        two_y = [t[r * HC : (r + 1) * HC, Y // 2 :] for r in range(HX)]
        at = 0
        for slot, group in enumerate(SLOTS):
            totals = []
            for row in pair(group):
                total = None
                for r in range(HX):
                    i = at * HX + r
                    if not used[i]:
                        continue
                    w2, w1 = tab[kind_of, 2 * i], tab[kind_of, 2 * i + 1]
                    term = jnp.where(even, w2, w1) * two_y[r] if row % 2 == 0 else w1 * one_y[r]
                    total = term if total is None else total + term
                totals.append(total)
                at += 1
            con[c, slot] = totals[0] if len(totals) == 1 else totals[0] + pltpu.roll(totals[1], 1, 1)
        for f in range(len(FLOWS)):
            for o in range(slabs):
                start(sum_copy(f, o, None, c))
        for o in range(slabs):
            @pl.when(g == o)
            def _():
                first, n = owned(FLOWS[0][1], o, part)
                got[c, o, 0:n] = con[c, first : first + n]

    def sum_copy(f, o, s, c):
        step, slots = FLOWS[f]
        first, n = owned(slots, o, part)
        if not n:
            return None
        here = sum(len(slots) for _, slots in FLOWS[:f]) + first
        copy = remote(
            con.at[c, pl.ds(here, n)], got.at[c, g if s is None else s, pl.ds(base[f], n)],
            cssem.at[f, o, c], crsem.at[f, g if s is None else s, c], (p + step, o),
        )
        return (reach[step] if step else g != o), (reach[-step] if step else g != s), copy

    def planar_part(c):
        for o in range(slabs):
            @pl.when(g == o)
            def _():
                for s in range(slabs):
                    total = [None] * part
                    for f, (_, slots) in enumerate(FLOWS):
                        arrive(sum_copy(f, o, s, c))
                    for f, (_, slots) in enumerate(FLOWS):
                        first, n = owned(slots, o, part)
                        for i in range(n):
                            slot = slots[first + i]
                            value = got[c, s, base[f] + i]
                            for at, row in enumerate(pair(slot)):
                                if row // part != o:
                                    continue
                                term = value
                                if isinstance(slot, tuple):
                                    term = pltpu.roll(value, Y // 2 - 1, 1) if at else value
                                    term = jnp.where(even, term, 0.0)
                                k = row - o * part
                                total[k] = term if total[k] is None else total[k] + term
                    at = s * (Z // 2) + c * HC
                    for k in range(part):
                        zfull[k, at : at + HC, :] = total[k]

    blocks = X // rows
    lax.fori_loop(0, blocks // 2, y_part, 0)
    flux_part(order[0])
    halo(3)
    for kind in range(4):
        start(z_copy(kind))
    lax.fori_loop(blocks // 2, blocks, y_part, 0)
    flux_part(order[1])
    z_part(HALO, Z - HALO, HALO, HALO + Z)
    flux_part(order[2])
    for c in loads[4:]:
        c.wait()
    finish_part(order[0])
    flux_part(order[3])
    finish_part(order[1])
    for kind in range(4):
        arrive(z_copy(kind))
    z_part(0, HALO, 0, 3 * HALO)
    z_part(Z - HALO, Z, Z - HALO, Z + 2 * HALO)
    finish_part(order[2])
    planar_part(order[0])
    finish_part(order[3])
    for n in range(1, NC):
        planar_part(order[n])
    for copy in stores:
        copy.wait()
    for kind in range(4):
        sent(z_copy(kind))
    for c in range(NC):
        for kind in range(5):
            sent(x_copy(kind, c))
        for f in range(len(FLOWS)):
            for o in range(slabs):
                sent(sum_copy(f, o, None, c))


def finish_kernel(pieces, field, planar, wz, next_out, coef_out, coef, sem):
    n = field.shape[0] // pieces
    copies = [
        pltpu.make_async_copy(field.at[pl.ds(i * n, n)], next_out.at[pl.ds(i * n, n)], sem.at[i])
        for i in range(pieces)
    ]
    for c in copies:
        c.start()
    for row in range(planar.shape[0]):
        coef[row] = jnp.dot(
            wz[...], planar[row], precision=HIGHEST, preferred_element_type=jnp.float32
        )
        copies.append(pltpu.make_async_copy(coef.at[row], coef_out.at[row], sem.at[pieces + row]))
        copies[-1].start()
    for c in copies:
        c.wait()


def pin(array):
    return pltpu.with_memory_space_constraint(jnp.asarray(array), pltpu.HBM)


def on_device(strips, slabs, previous, current, stiffness, buoyancy):
    X, Z, Y = current.shape
    NC, HX, HC = Z // CHUNK, X // 2, CHUNK // 2
    depth = slabs * Z // 2
    grad, div, lift = y_matrices(Y)
    hbm = pl.BlockSpec(memory_space=pltpu.HBM)
    part = HX // slabs
    places = sum(max(owned(slots, o, part)[1] for o in range(slabs)) for _, slots in FLOWS)
    table = x_table(strips, HX)
    used = tuple((table != 0).any(0).reshape(-1, 2).any(1).tolist())
    f32 = jnp.float32
    vmem = lambda *shape: pltpu.VMEM(shape, f32)
    dma = lambda *shape: pltpu.SemaphoreType.DMA(shape)
    field, planar = pl.pallas_call(
        functools.partial(kernel, strips, slabs, used),
        out_shape=(
            jax.ShapeDtypeStruct((X, Z, Y), f32),
            jax.ShapeDtypeStruct((HX // slabs, depth, Y // 2), f32),
        ),
        in_specs=[hbm] * 8,
        out_specs=(hbm, pl.BlockSpec(memory_space=pltpu.VMEM)),
        scratch_shapes=[
            vmem(X + 7, Z + 2 * HALO, Y),
            vmem(X + 1, Z + 2 * HALO, Y),
            vmem(X + 7, Z, Y),
            vmem(X, Z, Y),
            vmem(X, Z, Y),
            vmem(X, Z, Y),
            vmem(Y // 128, X, Z, 128),
            vmem(Y, Y),
            vmem(Y, Y),
            vmem(Y, Y),
            vmem(NC, len(SLOTS), HC, Y // 2),
            vmem(NC, slabs, places, HC, Y // 2),
            pltpu.SMEM(table.shape, f32),
            dma(8 + 2 * NC),
            dma(5, NC),
            dma(5, NC),
            dma(4),
            dma(4),
            dma(len(FLOWS), slabs, NC),
            dma(len(FLOWS), slabs, NC),
        ],
        compiler_params=pltpu.CompilerParams(
            collective_id=0, has_side_effects=True, vmem_limit_bytes=40 * 1024 * 1024
        ),
    )(
        pin(current), pin(previous), pin(stiffness), pin(buoyancy),
        pin(table), pin(grad), pin(div), pin(lift),
    )
    vspec = pl.BlockSpec(memory_space=pltpu.VMEM)
    pieces = 4
    return pl.pallas_call(
        functools.partial(finish_kernel, pieces),
        out_shape=(
            jax.ShapeDtypeStruct((X, Z, Y), f32),
            jax.ShapeDtypeStruct((part, depth, Y // 2), f32),
        ),
        in_specs=[pl.BlockSpec(memory_space=pl.ANY), vspec, vspec],
        out_specs=(pl.BlockSpec(memory_space=pl.ANY),) * 2,
        scratch_shapes=[vmem(part, depth, Y // 2), dma(pieces + part)],
        compiler_params=pltpu.CompilerParams(vmem_limit_bytes=16 * 1024 * 1024),
    )(field, planar, z_matrix(depth))


def solution(mesh):
    return jax.shard_map(
        functools.partial(on_device, mesh.shape["xy"], mesh.shape["gz"]),
        mesh=mesh,
        in_specs=(P("xy", "gz", None),) * 4,
        out_specs=(P("xy", "gz", None), P(("xy", "gz"), None, None)),
        check_vma=False,
    )
```
